256 devices in a mesh: leaf: 64 (over z, x, core), tile: 4 (over y).
Axes of the slice: x: 4, y: 4, z: 8, core: 2. Of those that a mesh axis runs over, the one named last changes fastest.
Arguments:
- top_sigma: float32 [2048, 2048], P(None, 'tile'), as said below
- anc_a: int32 [64, 12], P('leaf'), may hold values from 0 to 15, as said below
- u_a: float32 [64, 1536, 512], P('leaf'), may hold values from -0.15625 to 0.15625
- dinv_a: float32 [64, 512, 512], P('leaf', None, 'tile'), as said below
- parent: int32 [64], P('leaf'), may hold values from 0 to 63, as said below
- sel_b: int32 [64, 1, 8], P('leaf'), may hold values from 0 to 11, as said below
- pattern: int32 [64, 1, 12, 4], P('leaf'), may hold values 0 or 1
- u_b: float32 [64, 1, 1536, 512], P('leaf'), may hold values from -0.15625 to 0.15625
- dinv_b: float32 [64, 1, 512, 512], P('leaf', None, None, 'tile'), as said below
Outputs:
- sigma_a: float32 [64, 512, 512], P('leaf', None, 'tile')
- sigma_b: float32 [64, 1, 512, 512], P('leaf', None, None, 'tile')
The draws below stay inside these ranges and needn't reach their ends.
Inputs may be any that keep to these rules, and one draw needn't show every extreme that they name: parent never falls along the leaves, parent[l] <= l, parent[parent[l]] = parent[l], l - parent[l] < 4, some 4 consecutive leaves share one parent, and the last leaf is its own parent. `anc_a`: each row holds distinct tiles in rising order. `sel_b`: each row holds distinct positions in rising order. `top_sigma`: symmetric. `dinv_a`: each block symmetric. `dinv_b`: each block symmetric.
All inputs are finite; a program needn't handle non-finite values. No bound on the sum of `pattern` on one device may be relied on, other than what follows from the above.
Results may differ from the reference program's by a relative error of at most 0.0001.
Values sent between devices are 32-bit elements; how exact they have to be, the bound alone decides.
No kernel may reach another device: no remote copies, remote signals or barrier semaphores. Data moves between devices by JAX's collectives and lax.ppermute only.
A program may use at most 192 MiB of HBM per device.

```python
import jax
import jax.numpy as jnp
from jax import lax

TB = 128
WT = 4
TOPT = 16
NA = 12
NB = 8
MAXSEG = 4
BPD = 1
LEAVES = 64
W = 512
SA = 1536
SB = 1536
TOP = 2048


def symmetric_blocks(key, shape, order, off_scale):
    key_sym, key_diag = jax.random.split(key)
    base = jax.random.normal(key_sym, shape + (order, order), jnp.float32)
    sym = (base + jnp.swapaxes(base, -1, -2)) * (off_scale / jnp.sqrt(jnp.float32(order)))
    diag_vals = jax.random.uniform(key_diag, shape + (order,), jnp.float32, 0.5, 2.0)
    return sym + diag_vals[..., None] * jnp.eye(order, dtype=jnp.float32)


def draw_top_sigma(key, part):
    key = jax.random.fold_in(key, 3)
    key_main = jax.random.fold_in(key, 0)
    matrix = symmetric_blocks(key_main, (), TOP, 0.35)
    return matrix


def draw_dinv_a(key, part):
    key = jax.random.fold_in(key, 5)
    return symmetric_blocks(key, (LEAVES,), W, 0.3)


def draw_dinv_b(key, part):
    key = jax.random.fold_in(key, 7)
    return symmetric_blocks(key, (LEAVES, BPD), W, 0.3)


def distinct_sorted(key, rows, total, keep):
    keys = jax.random.split(key, rows)

    def one_row(row_key):
        return jnp.sort(jax.random.permutation(row_key, total)[:keep])
    return jax.vmap(one_row)(keys).astype(jnp.int32)


def draw_anc_a(key, part):
    key = jax.random.fold_in(key, 11)
    return distinct_sorted(key, LEAVES, TOPT, NA)


def draw_sel_b(key, part):
    key = jax.random.fold_in(key, 13)
    return distinct_sorted(key, LEAVES * BPD, NA, NB).reshape(LEAVES, BPD, NB)


def draw_parent(key, part):
    key = jax.random.fold_in(key, 17)
    key_len, key_pick = jax.random.split(key)
    run_lengths = jax.random.randint(key_len, (LEAVES,), 1, MAXSEG + 1)
    longest = jax.random.randint(key_pick, (), 0, 2)
    positions = jnp.arange(LEAVES, dtype=jnp.int32)
    run_lengths = jnp.where(positions == longest, MAXSEG, run_lengths)
    starts = jnp.cumsum(run_lengths) - run_lengths
    is_head = jnp.any(starts[None, :] == positions[:, None], axis=1)
    is_head = jnp.logical_or(is_head, positions == LEAVES - 1)
    return lax.cummax(jnp.where(is_head, positions, 0), axis=0).astype(jnp.int32)


def with_ends(values, key, least, top_value):
    longest = values.shape.index(max(values.shape))
    spots = []
    for shift in (0, 1):
        where = [jax.random.randint(jax.random.fold_in(key, axis), (), 0, length) for axis, length in enumerate(values.shape)]
        where[longest] = (where[longest] + shift) % values.shape[longest]
        spots.append(tuple(where))
    return values.at[spots[0]].set(least).at[spots[1]].set(top_value)


def level_of(rng, shape, pieces, smallest, top_value):
    level, own = 1.0, jax.random.fold_in(rng, 6)
    for position, shards_of in pieces:
        draws = jnp.exp(jax.random.uniform(jax.random.fold_in(own, position), (shards_of,), jnp.float32, smallest / len(pieces), top_value / len(pieces)))
        level = level * jnp.repeat(draws, shape[position] // shards_of).reshape([-1 if axis == position else 1 for axis in range(len(shape))])
    return level


def scatter_about(rng, dims, width, bound, cuts=(), kind=jnp.bfloat16):
    entries = width * jax.random.normal(rng, dims, jnp.float32)
    if cuts:
        entries = entries * level_of(rng, dims, cuts, -0.22, 0.18)
    return jnp.clip(entries, -bound, bound).astype(kind)


def setup_inputs(seed: int = 0) -> dict:
    arg_keys = jax.random.split(jax.random.key(seed), 10)
    return {
        "top_sigma": draw_top_sigma(jax.random.fold_in(arg_keys[9], 71), 0),
        "anc_a": draw_anc_a(jax.random.fold_in(arg_keys[9], 71), 0),
        "u_a": scatter_about(arg_keys[2], (LEAVES, SA, W), SA ** -0.5, 0.15625, ((0, 64),), jnp.float32),
        "dinv_a": draw_dinv_a(jax.random.fold_in(arg_keys[9], 71), 0),
        "parent": draw_parent(jax.random.fold_in(arg_keys[9], 71), 0),
        "sel_b": draw_sel_b(jax.random.fold_in(arg_keys[9], 71), 0),
        "pattern": with_ends((jax.random.randint(arg_keys[6], (LEAVES, BPD, WT + NB, WT), 0, 4) < 3).astype(jnp.int32), jax.random.fold_in(arg_keys[6], 1), 0, 1),
        "u_b": scatter_about(arg_keys[7], (LEAVES, BPD, SB, W), SB ** -0.5, 0.15625, ((0, 64),), jnp.float32),
        "dinv_b": draw_dinv_b(jax.random.fold_in(arg_keys[9], 71), 0),
    }


precise = lax.Precision.HIGHEST


def upper_level(top_tiles, ancestors, upper_factor, inverse_diag):
    top_block = jnp.take(jnp.take(top_tiles, ancestors, axis=0), ancestors, axis=2).reshape(SA, SA)
    cross_part = jnp.dot(top_block, upper_factor, precision=precise)
    own_block = inverse_diag + jnp.dot(upper_factor.T, cross_part, precision=precise)
    return own_block, jnp.concatenate([own_block, -cross_part], axis=0)


def reference(top_sigma, anc_a, u_a, dinv_a, parent, sel_b, pattern, u_b, dinv_b):
    top_tiles = top_sigma.reshape(TOPT, TB, TOPT, TB)

    def upper_one(leaf_args):
        return upper_level(top_tiles, leaf_args[0], leaf_args[1], leaf_args[2])

    sigma_a, extended = lax.map(upper_one, (anc_a, u_a, dinv_a))

    def lower_one(per_leaf):
        head_of, chosen_ids, marks, factor, inverse_diag = per_leaf
        extended_p = jnp.take(extended, head_of, axis=0).reshape(WT + NA, TB, W)
        parent_anc = jnp.take(anc_a, head_of, axis=0)
        blocks = []
        for index_b in range(BPD):
            tile_order = jnp.concatenate([jnp.arange(WT, dtype=jnp.int32), WT + chosen_ids[index_b]])
            side_rows = jnp.take(extended_p, tile_order, axis=0).reshape(SB, W)
            far_ids = jnp.take(parent_anc, chosen_ids[index_b])
            corner = jnp.take(jnp.take(top_tiles, far_ids, axis=0), far_ids, axis=2).reshape(NB * TB, NB * TB)
            right_cols = jnp.concatenate([side_rows[W:].T, corner], axis=0)
            full_block = jnp.concatenate([side_rows, right_cols], axis=1)
            tile_mask = jnp.repeat(jnp.repeat(marks[index_b].astype(jnp.float32), TB, axis=0), TB, axis=1)
            masked = factor[index_b] * tile_mask
            product = jnp.dot(full_block, masked, precision=precise)
            blocks.append(inverse_diag[index_b] + jnp.dot(masked.T, product, precision=precise))
        return jnp.stack(blocks)

    sigma_b = lax.map(lower_one, (parent, sel_b, pattern, u_b, dinv_b))
    return sigma_a, sigma_b
```

```python
import functools

import jax
import jax.numpy as jnp
from jax import lax
from jax.experimental import pallas as pl
from jax.experimental.pallas import tpu as pltpu
from jax.sharding import PartitionSpec as P

TB = 128
WT = 4
TOPT = 16
NA = 12
NB = 8
W = 512
SA = 1536
SB = 1536
OWN = 4
HALF = 256
F32 = jnp.float32
BF16 = jnp.bfloat16
VMEM_LIMIT = 48 * 1024 * 1024


def split(x):
    high = x.astype(BF16)
    return high, (x - high.astype(F32)).astype(BF16)


def dot3(a, b, contract):
    def one(u, v):
        return lax.dot_general(u, v, (contract, ((), ())), preferred_element_type=F32)

    return one(a[0], b[0]) + (one(a[0], b[1]) + one(a[1], b[0]))


FIRST = ((0,), (0,))
PLAIN = ((1,), (0,))


def upper_rows_kernel(info, g0, g1, g2, g3, u_ref, x_ref):
    step = pl.program_id(0)
    rows = jnp.concatenate([g0[...], g1[...], g2[...], g3[...]], axis=0)
    part = dot3(split(u_ref[0]), split(rows), FIRST)

    @pl.when(step == 0)
    def _():
        x_ref[...] = part

    @pl.when(step > 0)
    def _():
        x_ref[...] += part

    @pl.when(step == pl.num_programs(0) - 1)
    def _():
        for r in range(OWN):
            @pl.when(info[NA + OWN + r] == 0)
            def _():
                x_ref[:, r * TB:(r + 1) * TB] = jnp.zeros((W, TB), F32)


def upper_rows(info, top, u_a):
    def tile(i):
        return pl.BlockSpec((TB, W), lambda k, info: (info[4 * k + i], 0))

    return pl.pallas_call(
        upper_rows_kernel,
        grid_spec=pltpu.PrefetchScalarGridSpec(
            num_scalar_prefetch=1,
            grid=(3,),
            in_specs=[tile(0), tile(1), tile(2), tile(3), pl.BlockSpec((1, W, W), lambda k, info: (0, k, 0))],
            out_specs=pl.BlockSpec((W, W), lambda k, info: (0, 0)),
        ),
        out_shape=jax.ShapeDtypeStruct((W, W), F32),
        compiler_params=pltpu.CompilerParams(vmem_limit_bytes=VMEM_LIMIT),
        cost_estimate=pl.CostEstimate(flops=6 * SA * W * W, bytes_accessed=7 << 20, transcendentals=0),
        name="upper_rows",
    )(info, top, top, top, top, u_a)


def store_slabs(whole, place, slabs):
    for r in range(OWN):
        start = pl.multiple_of(lax.rem(place + r, OWN) * TB, TB)
        slabs[r][...] = whole[:, pl.ds(start, TB)]


def upper_sum_kernel(info, x_ref, u0, u1, u2, u3, s0, s1, s2, s3, whole):
    tiles = [jnp.where(info[NA + OWN + r] > 0, u[0], 0.0) for r, u in enumerate((u0, u1, u2, u3))]
    whole[...] = dot3(split(x_ref[...]), split(jnp.concatenate(tiles, axis=0)), PLAIN)
    store_slabs(whole, info[NA + 2 * OWN], (s0, s1, s2, s3))


def upper_sum(info, x, u_a):
    def tile(r):
        return pl.BlockSpec((1, TB, W), lambda k, info: (0, info[NA + r], 0))

    slab = pl.BlockSpec((W, TB), lambda k, info: (0, 0))
    return pl.pallas_call(
        upper_sum_kernel,
        grid_spec=pltpu.PrefetchScalarGridSpec(
            num_scalar_prefetch=1,
            grid=(1,),
            in_specs=[pl.BlockSpec((W, W), lambda k, info: (0, 0)), tile(0), tile(1), tile(2), tile(3)],
            out_specs=[slab] * 4,
            scratch_shapes=[pltpu.VMEM((W, W), F32)],
        ),
        out_shape=[jax.ShapeDtypeStruct((W, TB), F32)] * 4,
        compiler_params=pltpu.CompilerParams(vmem_limit_bytes=VMEM_LIMIT),
        cost_estimate=pl.CostEstimate(flops=6 * W * W * W, bytes_accessed=3 << 20, transcendentals=0),
        name="upper_sum",
    )(info, x, u_a, u_a, u_a, u_a)


def lower_prepare_kernel(info, *refs):
    g_refs, (u_ref, v_ref, u1h, u1l, u2h, u2l, e1h, e1l, masked) = refs[:NB], refs[NB:]
    mark = NB + 2 * OWN + 1
    for i in range(WT + NB):
        for j in range(WT):
            rows, cols = slice(i * TB, (i + 1) * TB), slice(j * TB, (j + 1) * TB)
            masked[rows, cols] = u_ref[0, 0, rows, cols] * info[mark + i * WT + j].astype(F32)
    near = masked[:W, :].T
    u1h[...], u1l[...] = split(near)
    start = pl.multiple_of(info[NB + 2 * OWN] * TB, TB)
    e1h[...], e1l[...] = split(masked[pl.ds(start, TB), :])
    for r in range(OWN):
        place = pl.multiple_of(W + info[NB + r] * TB, TB)
        own = jnp.where(info[NB + OWN + r] > 0, masked[pl.ds(place, TB), :], 0.0)
        u2h[r * TB:(r + 1) * TB, :], u2l[r * TB:(r + 1) * TB, :] = split(own)
    far = split(masked[W:, :])
    rows = split(jnp.concatenate([g[...] for g in g_refs], axis=0) * 0.5)
    v_ref[...] = dot3(far, rows, FIRST)


def lower_prepare(info, top, u_b):
    def tile(j):
        return pl.BlockSpec((TB, W), lambda k, info: (info[j], 0))

    def whole(rows, cols):
        return pl.BlockSpec((rows, cols), lambda k, info: (0, 0))

    return pl.pallas_call(
        lower_prepare_kernel,
        grid_spec=pltpu.PrefetchScalarGridSpec(
            num_scalar_prefetch=1,
            grid=(1,),
            in_specs=[tile(j) for j in range(NB)] + [pl.BlockSpec((1, 1, SB, W), lambda k, info: (0, 0, 0, 0))],
            out_specs=[whole(W, W)] * 5 + [whole(TB, W)] * 2,
            scratch_shapes=[pltpu.VMEM((SB, W), F32)],
        ),
        out_shape=[jax.ShapeDtypeStruct((W, W), F32)]
        + [jax.ShapeDtypeStruct((W, W), BF16)] * 4
        + [jax.ShapeDtypeStruct((TB, W), BF16)] * 2,
        compiler_params=pltpu.CompilerParams(vmem_limit_bytes=VMEM_LIMIT),
        cost_estimate=pl.CostEstimate(flops=6 * NB * TB * W * W, bytes_accessed=8 << 20, transcendentals=0),
        name="lower_prepare",
    )(info, *([top] * NB), u_b)


def fetch_parent(info, own, other, near, far, swapped, block, sems):
    core = info[1]
    mine = pl.ds(pl.multiple_of(core * HALF, HALF), HALF)
    rest = pl.ds(pl.multiple_of((1 - core) * HALF, HALF), HALF)

    def two(first, second):
        a = pltpu.make_async_copy(first, block.at[mine, :], sems.at[0])
        b = pltpu.make_async_copy(second, block.at[rest, :], sems.at[1])
        a.start()
        b.start()
        a.wait()
        b.wait()

    @pl.when(info[0] == 0)
    def _():
        two(own.at[mine, :], own.at[rest, :])

    @pl.when(info[0] == 1)
    def _():
        two(other.at[mine, :], other.at[rest, :])

    @pl.when(info[0] == 2)
    def _():
        two(near, swapped)

    @pl.when(info[0] == 3)
    def _():
        two(far, swapped)


def lower_cross_kernel(info, own, other, near, far, swapped, v_ref, u1h, u1l, u2h, u2l, p_ref, block, value, sems):
    fetch_parent(info, own, other, near, far, swapped, block, sems)
    value[...] = v_ref[...] - dot3((u1h[...], u1l[...]), split(block[...]), PLAIN)
    for r in range(OWN):
        @pl.when(info[3 + r] == 0)
        def _():
            value[:, r * TB:(r + 1) * TB] = jnp.zeros((W, TB), F32)
    product = dot3(split(value[...]), (u2h[...], u2l[...]), PLAIN)
    p_ref[...] = product + product.T


def lower_cross(info, five, prepared):
    whole = pl.BlockSpec((W, W), lambda k, info: (0, 0))
    return pl.pallas_call(
        lower_cross_kernel,
        grid_spec=pltpu.PrefetchScalarGridSpec(
            num_scalar_prefetch=1,
            grid=(1,),
            in_specs=[pl.BlockSpec(memory_space=pl.ANY)] * 5 + [whole] * 5,
            out_specs=whole,
            scratch_shapes=[pltpu.VMEM((W, W), F32), pltpu.VMEM((W, W), F32), pltpu.SemaphoreType.DMA((2,))],
        ),
        out_shape=jax.ShapeDtypeStruct((W, W), F32),
        compiler_params=pltpu.CompilerParams(vmem_limit_bytes=VMEM_LIMIT),
        cost_estimate=pl.CostEstimate(flops=12 * W * W * W, bytes_accessed=6 << 20, transcendentals=0),
        name="lower_cross",
    )(info, *five, *prepared)


def lower_sum_kernel(info, own, other, near, far, swapped, p_ref, u1h, u1l, e1h, e1l, s0, s1, s2, s3, block, whole, sems):
    fetch_parent(info, own, other, near, far, swapped, block, sems)
    inner = dot3((u1h[...], u1l[...]), split(block[...]), PLAIN)
    whole[...] = p_ref[...] + dot3(split(inner), (e1h[...], e1l[...]), PLAIN)
    store_slabs(whole, info[2], (s0, s1, s2, s3))


def lower_sum(info, five, p, u1h, u1l, e1h, e1l):
    def whole(rows, cols):
        return pl.BlockSpec((rows, cols), lambda k, info: (0, 0))

    return pl.pallas_call(
        lower_sum_kernel,
        grid_spec=pltpu.PrefetchScalarGridSpec(
            num_scalar_prefetch=1,
            grid=(1,),
            in_specs=[pl.BlockSpec(memory_space=pl.ANY)] * 5 + [whole(W, W)] * 3 + [whole(TB, W)] * 2,
            out_specs=[whole(W, TB)] * 4,
            scratch_shapes=[pltpu.VMEM((W, TB), F32), pltpu.VMEM((W, W), F32), pltpu.SemaphoreType.DMA((2,))],
        ),
        out_shape=[jax.ShapeDtypeStruct((W, TB), F32)] * 4,
        compiler_params=pltpu.CompilerParams(vmem_limit_bytes=VMEM_LIMIT),
        cost_estimate=pl.CostEstimate(flops=12 * W * W * TB, bytes_accessed=5 << 20, transcendentals=0),
        name="lower_sum",
    )(info, *five, p, u1h, u1l, e1h, e1l)


def sum_over_tiles(slabs, base, count):
    ways = [[(i, (i + r) % count) for i in range(count)] for r in range(count)]
    arrived = [lax.ppermute(slabs[r], "tile", ways[r]) for r in (2, 1, 3)]
    return base + ((slabs[0] + arrived[1]) + (arrived[0] + arrived[2]))


def body(top, anc_a, u_a, dinv_a, parent, sel_b, pattern, u_b, dinv_b):
    leaves = lax.axis_size("leaf")
    count = lax.axis_size("tile")
    place = lax.axis_index("tile").astype(jnp.int32)
    leaf = lax.axis_index("leaf").astype(jnp.int32)
    core = leaf % 2
    swap = [(i, i ^ 1) for i in range(leaves)]
    next_chip = [(i, i + 2) for i in range(leaves - 2)]
    chip_after = [(i, i + 4) for i in range(leaves - 4)]
    own_tiles = place * OWN + jnp.arange(OWN, dtype=jnp.int32)

    def places(tiles):
        same = own_tiles[:, None] == tiles[None, :]
        at = jnp.sum(jnp.where(same, jnp.arange(tiles.shape[0], dtype=jnp.int32), 0), axis=1)
        return at, jnp.any(same, axis=1).astype(jnp.int32)

    ancestors = anc_a[0]
    at_a, has_a = places(ancestors)
    info_a = jnp.concatenate([ancestors, at_a, has_a, place[None]])
    x = upper_rows(info_a, top, u_a)

    meta = jnp.concatenate([ancestors, parent, jnp.zeros((3,), jnp.int32)])
    meta = jnp.broadcast_to(jnp.pad(meta, (0, 112))[None], (8, 128))
    x, meta = lax.optimization_barrier((x, meta))
    meta_other = lax.ppermute(meta, "leaf", swap)
    even = core == 0
    meta_odd = jnp.where(even, meta_other, meta)
    meta_even = jnp.where(even, meta, meta_other)
    odd_heads = meta_odd[0, NA] == leaf - core + 1
    head = parent[0]
    back = leaf - head
    code = jnp.where(
        back == 0, 0, jnp.where(even, jnp.where(back == 3, 3, 2), jnp.where(back == 1, 1, 2))
    ).astype(jnp.int32)
    even_back = leaf - core - meta_even[0, NA]
    swap_far = jnp.logical_and(jnp.logical_not(even), even_back == 3)

    def send(block):
        other = lax.ppermute(block, "leaf", swap)
        mine = lax.dynamic_slice_in_dim(block, core * HALF, HALF, 0)
        others = lax.dynamic_slice_in_dim(other, core * HALF, HALF, 0)
        odd = jnp.where(even, others, mine)
        latest = jnp.where(jnp.logical_xor(even, odd_heads), mine, others)
        near = lax.ppermute(latest, "leaf", next_chip)
        far = lax.ppermute(odd, "leaf", chip_after)
        return other, near, far

    def receive(block, sent):
        other, near, far = sent
        swapped = lax.ppermute(jnp.where(swap_far, far, near), "leaf", swap)
        return block, other, near, far, swapped

    sent_x = send(x)
    meta_near = lax.ppermute(jnp.where(odd_heads, meta_odd, meta_even), "leaf", next_chip)
    meta_far = lax.ppermute(meta_odd, "leaf", chip_after)
    parent_anc = jnp.where(
        code == 0, meta, jnp.where(code == 1, meta_other, jnp.where(code == 2, meta_near, meta_far))
    )[0, :NA]

    slabs_a = upper_sum(info_a, x, u_a)
    sigma_a = sum_over_tiles(slabs_a, dinv_a[0], count)
    sent_s = send(sigma_a)

    chosen = sel_b[0, 0]
    far_tiles = jnp.sum(
        jnp.where(chosen[:, None] == jnp.arange(NA, dtype=jnp.int32)[None], parent_anc[None], 0), axis=1
    )
    at_b, has_b = places(far_tiles)
    info_b = jnp.concatenate([far_tiles, at_b, has_b, place[None], pattern.reshape(-1)])
    v, u1h, u1l, u2h, u2l, e1h, e1l = lower_prepare(info_b, top, u_b)

    info_c = jnp.concatenate([jnp.stack([code, core, place]), has_b])
    p = lower_cross(info_c, receive(x, sent_x), (v, u1h, u1l, u2h, u2l))
    slabs_b = lower_sum(info_c, receive(sigma_a, sent_s), p, u1h, u1l, e1h, e1l)
    sigma_b = sum_over_tiles(slabs_b, dinv_b[0, 0], count)
    return sigma_a[None], sigma_b[None, None]


def solution(mesh):
    in_specs = (
        P(None, "tile"),
        P("leaf", None),
        P("leaf", None, None),
        P("leaf", None, "tile"),
        P("leaf"),
        P("leaf", None, None),
        P("leaf", None, None, None),
        P("leaf", None, None, None),
        P("leaf", None, None, "tile"),
    )
    out_specs = (P("leaf", None, "tile"), P("leaf", None, None, "tile"))
    return jax.shard_map(body, mesh=mesh, in_specs=in_specs, out_specs=out_specs, check_vma=False)
```

```python
import jax
import jax.numpy as jnp
from jax import lax
from jax.experimental import pallas as pl
from jax.experimental.pallas import tpu as pltpu
from jax.sharding import PartitionSpec as P

TB = 128
WT = 4
NA = 12
NB = 8
W = 512
SA = 1536
SB = 1536
OWN = 4
HALF = 256
SENT = HALF + 8
BLOCK = 2 * SENT
CHUNKS = 3
F32 = jnp.float32
BF16 = jnp.bfloat16
FIRST = ((0,), (0,))
PLAIN = ((1,), (0,))
ANY = pl.BlockSpec(memory_space=pl.ANY)


def split(x):
    high = x.astype(BF16)
    return high, (x - high.astype(F32)).astype(BF16)


def dot3(a, b, contract):
    def one(u, v):
        return lax.dot_general(u, v, (contract, ((), ())), preferred_element_type=F32)

    return one(a[0], b[0]) + (one(a[0], b[1]) + one(a[1], b[0]))


HELD = pl.BlockSpec(memory_space=pltpu.VMEM)


def whole(*shape):
    return pl.BlockSpec(shape, lambda *_: (0,) * len(shape))


def call(kernel, name, scalars, in_specs, operands, out_shapes, scratch=(), limit=24, out=HELD):
    many = isinstance(out_shapes, list)
    out_specs = [out] * len(out_shapes) if many else out
    return pl.pallas_call(
        kernel,
        grid_spec=pltpu.PrefetchScalarGridSpec(
            num_scalar_prefetch=len(scalars),
            grid=(1,),
            in_specs=in_specs,
            out_specs=out_specs,
            scratch_shapes=list(scratch),
        ),
        out_shape=out_shapes,
        compiler_params=pltpu.CompilerParams(vmem_limit_bytes=limit << 20),
        cost_estimate=pl.CostEstimate(flops=1 << 20, bytes_accessed=1 << 16, transcendentals=0),
        name=name,
    )(*scalars, *operands)


def f32(*shape):
    return jax.ShapeDtypeStruct(shape, F32)


def bf16(*shape):
    return jax.ShapeDtypeStruct(shape, BF16)


def place_among(tiles, count, tile):
    at, there = jnp.int32(0), jnp.int32(0)
    for j in range(count):
        same = (tiles(j) == tile).astype(jnp.int32)
        at, there = at + j * same, there + same
    return at, there


def store_slabs(full, place, slabs):
    for r in range(OWN):
        start = pl.multiple_of(lax.rem(place + r, OWN) * TB, TB)
        slabs[r][...] = full[:, pl.ds(start, TB)]


def halves(core):
    mine = pl.ds(pl.multiple_of(core * HALF, HALF), HALF)
    rest = pl.ds(pl.multiple_of((1 - core) * HALF, HALF), HALF)
    return mine, rest


def upper_rows_kernel(anc, parent, others_parent, where, top, u_ref, block, rows, factor, total, row_sems, u_sems):
    per = NA // CHUNKS
    size = per * TB

    def u_copy(c):
        part = pl.ds(c * size, size)
        return pltpu.make_async_copy(u_ref.at[0, part, :], factor.at[part, :], u_sems.at[c])

    def row_copy(j):
        start = pl.multiple_of(anc[0, j] * TB, TB)
        return pltpu.make_async_copy(top.at[pl.ds(start, TB), :], rows.at[pl.ds(j * TB, TB), :], row_sems.at[j])

    for c in range(CHUNKS):
        u_copy(c).start()
        for i in range(per):
            row_copy(c * per + i).start()
    for c in range(CHUNKS):
        u_copy(c).wait()
        for i in range(per):
            row_copy(c * per + i).wait()
        part = slice(c * size, (c + 1) * size)
        product = dot3(split(factor[part, :]), split(rows[part, :]), FIRST)
        if c == 0:
            total[...] = product
        else:
            total[...] += product
    for r in range(OWN):
        _, there = place_among(lambda j: anc[0, j], NA, where[0] * OWN + r)

        @pl.when(there == 0)
        def _():
            total[:, r * TB:(r + 1) * TB] = jnp.zeros((W, TB), F32)

    lane = lax.broadcasted_iota(jnp.int32, (SENT - HALF, W), 1)
    marks = jnp.where(lane == NA, parent[0], jnp.where(lane == NA + 1, others_parent[0], 0))
    for j in range(NA):
        marks = jnp.where(lane == j, anc[0, j], marks)
    for h in range(2):
        block[h * SENT:h * SENT + HALF, :] = total[h * HALF:(h + 1) * HALF, :]
        block[h * SENT + HALF:(h + 1) * SENT, :] = marks.astype(F32)


def upper_sum_kernel(anc, where, block, u_ref, s0, s1, s2, s3, tiles, full, sems):
    def copy(r, at):
        rows = pl.ds(pl.multiple_of(at * TB, TB), TB)
        return pltpu.make_async_copy(u_ref.at[0, rows, :], tiles.at[pl.ds(r * TB, TB), :], sems.at[r])

    found = [place_among(lambda j: anc[0, j], NA, where[0] * OWN + r) for r in range(OWN)]
    for r in range(OWN):
        copy(r, found[r][0]).start()
    for r in range(OWN):
        copy(r, found[r][0]).wait()
    own = split(
        jnp.concatenate(
            [jnp.where(found[r][1] > 0, tiles[r * TB:(r + 1) * TB, :], 0.0) for r in range(OWN)], axis=0
        )
    )
    for h in range(2):
        full[h * HALF:(h + 1) * HALF, :] = dot3(split(block[h * SENT:h * SENT + HALF, :]), own, PLAIN)
    store_slabs(full, where[0], (s0, s1, s2, s3))


def lower_prepare_kernel(pattern, u_ref, high, low):
    for i in range(WT + NB):
        for j in range(WT):
            rows, cols = slice(i * TB, (i + 1) * TB), slice(j * TB, (j + 1) * TB)
            masked = u_ref[0, 0, rows, cols] * pattern[i * WT + j].astype(F32)
            high[rows, cols], low[rows, cols] = split(masked)


def after_kernel(array, earlier, same):
    pass


def after(array, earlier):
    return pl.pallas_call(
        after_kernel,
        in_specs=[ANY, ANY],
        out_specs=ANY,
        out_shape=jax.ShapeDtypeStruct(array.shape, array.dtype),
        input_output_aliases={0: 0},
        cost_estimate=pl.CostEstimate(flops=1, bytes_accessed=1, transcendentals=0),
        name="after",
    )(array, earlier)


def take_marks_kernel(array, same, marks, sem):
    copy = pltpu.make_async_copy(array.at[pl.ds(HALF, SENT - HALF), :], marks, sem)
    copy.start()
    copy.wait()


def take_marks(array):
    return pl.pallas_call(
        take_marks_kernel,
        in_specs=[ANY],
        out_specs=[ANY, HELD],
        out_shape=[jax.ShapeDtypeStruct(array.shape, F32), f32(SENT - HALF, W)],
        scratch_shapes=[pltpu.SemaphoreType.DMA],
        input_output_aliases={0: 0},
        cost_estimate=pl.CostEstimate(flops=1, bytes_accessed=1, transcendentals=0),
        name="take_marks",
    )(array)


def fetch(choice, copies):
    for c, some in enumerate(copies):
        @pl.when(choice == c)
        def _():
            for copy in some:
                copy.start()
            for copy in some:
                copy.wait()


def lower_cross_kernel(code, where, far_tiles, own, other, near, swapped, far, *refs):
    high, low, p_ref, block, value, sems = refs[NB:]
    mine, rest = halves(where[1])
    part = pl.ds(0, HALF)
    second = pl.ds(SENT, HALF)

    def full(ref):
        return [
            pltpu.make_async_copy(ref.at[part, :], block.at[pl.ds(0, HALF), :], sems.at[0]),
            pltpu.make_async_copy(ref.at[second, :], block.at[pl.ds(HALF, HALF), :], sems.at[1]),
        ]

    fetch(
        code[0],
        [
            full(own),
            full(other),
            [
                pltpu.make_async_copy(near.at[part, :], block.at[mine, :], sems.at[0]),
                pltpu.make_async_copy(swapped.at[part, :], block.at[rest, :], sems.at[1]),
            ],
            full(far),
        ],
    )
    rows = split(jnp.concatenate([g[...] for g in refs[:NB]], axis=0) * 0.5)
    value[...] = dot3((high[W:, :], low[W:, :]), rows, FIRST) - dot3((high[:W, :], low[:W, :]), split(block[...]), FIRST)
    own_high, own_low = [], []
    for r in range(OWN):
        at, there = place_among(lambda j: far_tiles[j], NB, where[0] * OWN + r)

        @pl.when(there == 0)
        def _():
            value[:, r * TB:(r + 1) * TB] = jnp.zeros((W, TB), F32)

        rows = pl.ds(pl.multiple_of(W + at * TB, TB), TB)
        own_high.append(high[rows, :])
        own_low.append(low[rows, :])
    rows_of_own = jnp.concatenate(own_high, axis=0), jnp.concatenate(own_low, axis=0)
    product = dot3(split(value[...]), rows_of_own, PLAIN)
    p_ref[...] = product + product.T


def lower_sum_kernel(code, where, own, even, near, swapped, far, p_ref, high, low, s0, s1, s2, s3, block, full, sem):
    fetch(code[1], [[pltpu.make_async_copy(ref, block, sem)] for ref in (own, even, near, swapped, far)])
    inner = dot3(split(block[...]), (high[:W, :], low[:W, :]), FIRST)
    rows = pl.ds(pl.multiple_of(where[0] * TB, TB), TB)
    full[...] = p_ref[...] + dot3(split(inner), (high[rows, :], low[rows, :]), FIRST)
    store_slabs(full, where[0], (s0, s1, s2, s3))


def to_owners(slabs, count):
    ways = [[(i, (i + r) % count) for i in range(count)] for r in range(count)]
    arrived = [lax.ppermute(slabs[r], "tile", ways[r]) for r in (2, 1, 3)]
    return slabs[0], arrived[1], arrived[0], arrived[2]


def body(top, anc_a, u_a, dinv_a, parent, sel_b, pattern, u_b, dinv_b):
    leaves = lax.axis_size("leaf")
    count = lax.axis_size("tile")
    place = lax.axis_index("tile").astype(jnp.int32)
    leaf = lax.axis_index("leaf").astype(jnp.int32)
    core = leaf % 2
    even = core == 0
    where = jnp.stack([place, core, leaf])
    swap = [(i, i ^ 1) for i in range(leaves)]
    next_chip = [(i, i + 2) for i in range(leaves - 2)]
    crossing = [(i, (i + 2) ^ 1) for i in range(leaves - 2)]
    odd_on = [(i, i + 3) for i in range(1, leaves - 3, 2)]

    others_parent = lax.ppermute(parent, "leaf", swap)
    block = call(
        upper_rows_kernel, "upper_rows", (anc_a, parent, others_parent, where), [ANY, ANY], (top, u_a), f32(BLOCK, W),
        [pltpu.VMEM((SA, W), F32), pltpu.VMEM((SA, W), F32), pltpu.VMEM((W, W), F32),
         pltpu.SemaphoreType.DMA((NA,)), pltpu.SemaphoreType.DMA((CHUNKS,))],
    )
    slabs_a = call(
        upper_sum_kernel, "upper_sum", (anc_a, where), [HELD, ANY], (block, u_a), [f32(W, TB)] * 4,
        [pltpu.VMEM((W, W), F32), pltpu.VMEM((W, W), F32), pltpu.SemaphoreType.DMA((OWN,))],
    )
    other = lax.ppermute(block, "leaf", swap)
    odd_heads = jnp.where(even, others_parent[0], parent[0]) == leaf - core + 1
    latest = jnp.where(
        jnp.logical_xor(even, odd_heads),
        lax.dynamic_slice_in_dim(block, core * SENT, SENT, 0),
        lax.dynamic_slice_in_dim(other, core * SENT, SENT, 0),
    )
    near = lax.ppermute(latest, "leaf", next_chip)
    far = lax.ppermute(block, "leaf", odd_on)

    high, low = call(
        lower_prepare_kernel, "lower_prepare", (pattern.reshape(-1),), [whole(1, 1, SB, W)], (u_b,), [bf16(SB, W)] * 2,
    )
    own, next_one, opposite, last_one = to_owners(slabs_a, count)
    sigma_a = dinv_a[0] + ((own + next_one) + (opposite + last_one))
    near_s = lax.ppermute(sigma_a, "leaf", crossing)
    far_s = lax.ppermute(sigma_a, "leaf", odd_on)

    head = parent[0]
    back = leaf - head
    from_far = jnp.logical_and(even, back == 3)
    from_even = jnp.logical_and(jnp.logical_not(even), back == 1)
    code_x = jnp.where(back == 0, 0, jnp.where(from_even, 1, jnp.where(from_far, 3, 2)))
    direct = jnp.where(head % 2 == 1 - core, 2, 3)
    code_s = jnp.where(back == 0, 0, jnp.where(from_even, 1, jnp.where(from_far, 4, direct)))
    code = jnp.stack([code_x, code_s]).astype(jnp.int32)

    near, near_marks = take_marks(after(near, sigma_a))
    swapped = lax.ppermute(near, "leaf", swap)
    marked = jnp.where(
        code_x == 0, block[HALF:SENT], jnp.where(code_x == 1, other[HALF:SENT], jnp.where(code_x == 3, far[HALF:SENT], near_marks))
    )[0, :NA].astype(jnp.int32)
    far_tiles = jnp.sum(
        jnp.where(sel_b[0, 0][:, None] == jnp.arange(NA, dtype=jnp.int32)[None], marked[None], 0), axis=1
    )
    p = call(
        lower_cross_kernel, "lower_cross", (code, where, far_tiles),
        [ANY] * 5 + [pl.BlockSpec((TB, W), lambda k, code, where, tiles, j=j: (tiles[j], 0)) for j in range(NB)] + [HELD] * 2,
        (block, other, near, swapped, far) + (top,) * NB + (high, low),
        f32(W, W), [pltpu.VMEM((W, W), F32), pltpu.VMEM((W, W), F32), pltpu.SemaphoreType.DMA((2,))],
    )
    near_s = after(near_s, far_s)
    swapped_s = lax.ppermute(near_s, "leaf", swap)
    other_s = lax.ppermute(sigma_a, "leaf", swap)
    slabs_b = call(
        lower_sum_kernel, "lower_sum", (code, where), [ANY] * 5 + [HELD] * 3,
        (sigma_a, other_s, near_s, swapped_s, far_s, p, high, low), [f32(W, TB)] * 4,
        [pltpu.VMEM((W, TB), F32), pltpu.VMEM((W, W), F32), pltpu.SemaphoreType.DMA],
    )
    own, next_one, opposite, last_one = to_owners(slabs_b, count)
    sigma_b = dinv_b + ((own + next_one) + (opposite + last_one))[None, None]
    return sigma_a[None], sigma_b


def solution(mesh):
    in_specs = (
        P(None, "tile"),
        P("leaf", None),
        P("leaf", None, None),
        P("leaf", None, "tile"),
        P("leaf"),
        P("leaf", None, None),
        P("leaf", None, None, None),
        P("leaf", None, None, None),
        P("leaf", None, None, "tile"),
    )
    out_specs = (P("leaf", None, "tile"), P("leaf", None, None, "tile"))
    return jax.shard_map(body, mesh=mesh, in_specs=in_specs, out_specs=out_specs, check_vma=False)
```

```python
import jax
import jax.numpy as jnp
from jax import lax
from jax.experimental import pallas as pl
from jax.experimental.pallas import tpu as pltpu
from jax.sharding import PartitionSpec as P

TB = 128
WT = 4
NA = 12
NB = 8
W = 512
SA = 1536
SB = 1536
OWN = 4
HALF = 256
SENT = HALF + 8
BLOCK = 2 * SENT
CHUNKS = 3
F32 = jnp.float32
BF16 = jnp.bfloat16
FIRST = ((0,), (0,))
PLAIN = ((1,), (0,))
ANY = pl.BlockSpec(memory_space=pl.ANY)


def split(x):
    high = x.astype(BF16)
    return high, (x - high.astype(F32)).astype(BF16)


def dot3(a, b, contract):
    def one(u, v):
        return lax.dot_general(u, v, (contract, ((), ())), preferred_element_type=F32)

    return one(a[0], b[0]) + (one(a[0], b[1]) + one(a[1], b[0]))


HELD = pl.BlockSpec(memory_space=pltpu.VMEM)


def whole(*shape):
    return pl.BlockSpec(shape, lambda *_: (0,) * len(shape))


def call(kernel, name, scalars, in_specs, operands, out_shapes, scratch=(), limit=24, out=HELD):
    many = isinstance(out_shapes, list)
    out_specs = [out] * len(out_shapes) if many else out
    return pl.pallas_call(
        kernel,
        grid_spec=pltpu.PrefetchScalarGridSpec(
            num_scalar_prefetch=len(scalars),
            grid=(1,),
            in_specs=in_specs,
            out_specs=out_specs,
            scratch_shapes=list(scratch),
        ),
        out_shape=out_shapes,
        compiler_params=pltpu.CompilerParams(vmem_limit_bytes=limit << 20),
        cost_estimate=pl.CostEstimate(flops=1 << 20, bytes_accessed=1 << 16, transcendentals=0),
        name=name,
    )(*scalars, *operands)


def f32(*shape):
    return jax.ShapeDtypeStruct(shape, F32)


def bf16(*shape):
    return jax.ShapeDtypeStruct(shape, BF16)


def place_among(tiles, count, tile):
    at, there = jnp.int32(0), jnp.int32(0)
    for j in range(count):
        same = (tiles(j) == tile).astype(jnp.int32)
        at, there = at + j * same, there + same
    return at, there


def store_slabs(full, place, slabs):
    for r in range(OWN):
        start = pl.multiple_of(lax.rem(place + r, OWN) * TB, TB)
        slabs[r][...] = full[:, pl.ds(start, TB)]


def halves(core):
    mine = pl.ds(pl.multiple_of(core * HALF, HALF), HALF)
    rest = pl.ds(pl.multiple_of((1 - core) * HALF, HALF), HALF)
    return mine, rest


def upper_rows_kernel(anc, parent, others_parent, where, top, u_ref, block, rows, factor, total, row_sems, u_sems):
    per = NA // CHUNKS
    size = per * TB

    def u_copy(c):
        part = pl.ds(c * size, size)
        return pltpu.make_async_copy(u_ref.at[0, part, :], factor.at[part, :], u_sems.at[c])

    def row_copy(j):
        start = pl.multiple_of(anc[0, j] * TB, TB)
        return pltpu.make_async_copy(top.at[pl.ds(start, TB), :], rows.at[pl.ds(j * TB, TB), :], row_sems.at[j])

    for c in range(CHUNKS):
        u_copy(c).start()
        for i in range(per):
            row_copy(c * per + i).start()
    for c in range(CHUNKS):
        u_copy(c).wait()
        for i in range(per):
            row_copy(c * per + i).wait()
        part = slice(c * size, (c + 1) * size)
        product = dot3(split(factor[part, :]), split(rows[part, :]), FIRST)
        if c == 0:
            total[...] = product
        else:
            total[...] += product
    for r in range(OWN):
        _, there = place_among(lambda j: anc[0, j], NA, where[0] * OWN + r)

        @pl.when(there == 0)
        def _():
            total[:, r * TB:(r + 1) * TB] = jnp.zeros((W, TB), F32)

    lane = lax.broadcasted_iota(jnp.int32, (SENT - HALF, W), 1)
    marks = jnp.where(lane == NA, parent[0], jnp.where(lane == NA + 1, others_parent[0], 0))
    for j in range(NA):
        marks = jnp.where(lane == j, anc[0, j], marks)
    for h in range(2):
        block[h * SENT:h * SENT + HALF, :] = total[h * HALF:(h + 1) * HALF, :]
        block[h * SENT + HALF:(h + 1) * SENT, :] = marks.astype(F32)


def upper_sum_kernel(anc, where, block, u_ref, s0, s1, s2, s3, tiles, full, sems):
    def copy(r, at):
        rows = pl.ds(pl.multiple_of(at * TB, TB), TB)
        return pltpu.make_async_copy(u_ref.at[0, rows, :], tiles.at[pl.ds(r * TB, TB), :], sems.at[r])

    found = [place_among(lambda j: anc[0, j], NA, where[0] * OWN + r) for r in range(OWN)]
    for r in range(OWN):
        copy(r, found[r][0]).start()
    for r in range(OWN):
        copy(r, found[r][0]).wait()
    own = split(
        jnp.concatenate(
            [jnp.where(found[r][1] > 0, tiles[r * TB:(r + 1) * TB, :], 0.0) for r in range(OWN)], axis=0
        )
    )
    for h in range(2):
        full[h * HALF:(h + 1) * HALF, :] = dot3(split(block[h * SENT:h * SENT + HALF, :]), own, PLAIN)
    store_slabs(full, where[0], (s0, s1, s2, s3))


def lower_prepare_kernel(pattern, u_ref, high, low):
    for i in range(WT + NB):
        for j in range(WT):
            rows, cols = slice(i * TB, (i + 1) * TB), slice(j * TB, (j + 1) * TB)
            masked = u_ref[0, 0, rows, cols] * pattern[i * WT + j].astype(F32)
            high[rows, cols], low[rows, cols] = split(masked)


def after_kernel(array, earlier, same):
    pass


def after(array, earlier):
    return pl.pallas_call(
        after_kernel,
        in_specs=[ANY, ANY],
        out_specs=ANY,
        out_shape=jax.ShapeDtypeStruct(array.shape, array.dtype),
        input_output_aliases={0: 0},
        compiler_params=pltpu.CompilerParams(vmem_limit_bytes=1 << 20),
        cost_estimate=pl.CostEstimate(flops=1, bytes_accessed=1, transcendentals=0),
        name="after",
    )(array, earlier)


def take_marks_kernel(array, same, marks, sem):
    copy = pltpu.make_async_copy(array.at[pl.ds(HALF, SENT - HALF), :], marks, sem)
    copy.start()
    copy.wait()


def take_marks(array):
    return pl.pallas_call(
        take_marks_kernel,
        in_specs=[ANY],
        out_specs=[ANY, HELD],
        out_shape=[jax.ShapeDtypeStruct(array.shape, F32), f32(SENT - HALF, W)],
        scratch_shapes=[pltpu.SemaphoreType.DMA],
        input_output_aliases={0: 0},
        compiler_params=pltpu.CompilerParams(vmem_limit_bytes=1 << 20),
        cost_estimate=pl.CostEstimate(flops=1, bytes_accessed=1, transcendentals=0),
        name="take_marks",
    )(array)


def fetch(choice, copies):
    for c, some in enumerate(copies):
        @pl.when(choice == c)
        def _():
            for copy in some:
                copy.start()
            for copy in some:
                copy.wait()


def lower_cross_kernel(code, where, far_tiles, own, other, near, swapped, far, *refs):
    high, low, p_ref, block, value, sems = refs[NB:]
    mine, rest = halves(where[1])
    part = pl.ds(0, HALF)
    second = pl.ds(SENT, HALF)

    def full(ref):
        return [
            pltpu.make_async_copy(ref.at[part, :], block.at[pl.ds(0, HALF), :], sems.at[0]),
            pltpu.make_async_copy(ref.at[second, :], block.at[pl.ds(HALF, HALF), :], sems.at[1]),
        ]

    fetch(
        code[0],
        [
            full(own),
            full(other),
            [
                pltpu.make_async_copy(near.at[part, :], block.at[mine, :], sems.at[0]),
                pltpu.make_async_copy(swapped.at[part, :], block.at[rest, :], sems.at[1]),
            ],
            full(far),
        ],
    )
    rows = split(jnp.concatenate([g[...] for g in refs[:NB]], axis=0) * 0.5)
    value[...] = dot3((high[W:, :], low[W:, :]), rows, FIRST) - dot3((high[:W, :], low[:W, :]), split(block[...]), FIRST)
    own_high, own_low = [], []
    for r in range(OWN):
        at, there = place_among(lambda j: far_tiles[j], NB, where[0] * OWN + r)

        @pl.when(there == 0)
        def _():
            value[:, r * TB:(r + 1) * TB] = jnp.zeros((W, TB), F32)

        rows = pl.ds(pl.multiple_of(W + at * TB, TB), TB)
        own_high.append(high[rows, :])
        own_low.append(low[rows, :])
    rows_of_own = jnp.concatenate(own_high, axis=0), jnp.concatenate(own_low, axis=0)
    product = dot3(split(value[...]), rows_of_own, PLAIN)
    p_ref[...] = product + product.T


def lower_sum_kernel(code, where, own, even, near, swapped, far, p_ref, high, low, s0, s1, s2, s3, block, full, sem):
    fetch(code[1], [[pltpu.make_async_copy(ref, block, sem)] for ref in (own, even, near, swapped, far)])
    inner = dot3(split(block[...]), (high[:W, :], low[:W, :]), FIRST)
    rows = pl.ds(pl.multiple_of(where[0] * TB, TB), TB)
    full[...] = p_ref[...] + dot3(split(inner), (high[rows, :], low[rows, :]), FIRST)
    store_slabs(full, where[0], (s0, s1, s2, s3))


def to_owners(slabs, count):
    ways = [[(i, (i + r) % count) for i in range(count)] for r in range(count)]
    arrived = [lax.ppermute(slabs[r], "tile", ways[r]) for r in (2, 1, 3)]
    return slabs[0], arrived[1], arrived[0], arrived[2]


def body(top, anc_a, u_a, dinv_a, parent, sel_b, pattern, u_b, dinv_b):
    leaves = lax.axis_size("leaf")
    count = lax.axis_size("tile")
    place = lax.axis_index("tile").astype(jnp.int32)
    leaf = lax.axis_index("leaf").astype(jnp.int32)
    core = leaf % 2
    even = core == 0
    where = jnp.stack([place, core, leaf])
    swap = [(i, i ^ 1) for i in range(leaves)]
    next_chip = [(i, i + 2) for i in range(leaves - 2)]
    crossing = [(i, (i + 2) ^ 1) for i in range(leaves - 2)]
    odd_on = [(i, i + 3) for i in range(1, leaves - 3, 2)]

    others_parent = lax.ppermute(parent, "leaf", swap)
    block = call(
        upper_rows_kernel, "upper_rows", (anc_a, parent, others_parent, where), [ANY, ANY], (top, u_a), f32(BLOCK, W),
        [pltpu.VMEM((SA, W), F32), pltpu.VMEM((SA, W), F32), pltpu.VMEM((W, W), F32),
         pltpu.SemaphoreType.DMA((NA,)), pltpu.SemaphoreType.DMA((CHUNKS,))], 58,
    )
    slabs_a = call(
        upper_sum_kernel, "upper_sum", (anc_a, where), [HELD, ANY], (block, u_a), [f32(W, TB)] * 4,
        [pltpu.VMEM((W, W), F32), pltpu.VMEM((W, W), F32), pltpu.SemaphoreType.DMA((OWN,))],
    )
    other = lax.ppermute(block, "leaf", swap)
    odd_heads = jnp.where(even, others_parent[0], parent[0]) == leaf - core + 1
    latest = jnp.where(
        jnp.logical_xor(even, odd_heads),
        lax.dynamic_slice_in_dim(block, core * SENT, SENT, 0),
        lax.dynamic_slice_in_dim(other, core * SENT, SENT, 0),
    )
    near = lax.ppermute(latest, "leaf", next_chip)
    far = lax.ppermute(block, "leaf", odd_on)

    high, low = call(
        lower_prepare_kernel, "lower_prepare", (pattern.reshape(-1),), [whole(1, 1, SB, W)], (u_b,), [bf16(SB, W)] * 2,
    )
    own, next_one, opposite, last_one = to_owners(slabs_a, count)
    sigma_a = dinv_a[0] + ((own + next_one) + (opposite + last_one))
    near_s = lax.ppermute(sigma_a, "leaf", crossing)
    far_s = lax.ppermute(sigma_a, "leaf", odd_on)

    head = parent[0]
    back = leaf - head
    from_far = jnp.logical_and(even, back == 3)
    from_even = jnp.logical_and(jnp.logical_not(even), back == 1)
    code_x = jnp.where(back == 0, 0, jnp.where(from_even, 1, jnp.where(from_far, 3, 2)))
    direct = jnp.where(head % 2 == 1 - core, 2, 3)
    code_s = jnp.where(back == 0, 0, jnp.where(from_even, 1, jnp.where(from_far, 4, direct)))
    code = jnp.stack([code_x, code_s]).astype(jnp.int32)

    near, near_marks = take_marks(after(near, sigma_a))
    swapped = lax.ppermute(near, "leaf", swap)
    marked = jnp.where(
        code_x == 0, block[HALF:SENT], jnp.where(code_x == 1, other[HALF:SENT], jnp.where(code_x == 3, far[HALF:SENT], near_marks))
    )[0, :NA].astype(jnp.int32)
    far_tiles = jnp.sum(
        jnp.where(sel_b[0, 0][:, None] == jnp.arange(NA, dtype=jnp.int32)[None], marked[None], 0), axis=1
    )
    p = call(
        lower_cross_kernel, "lower_cross", (code, where, far_tiles),
        [ANY] * 5 + [pl.BlockSpec((TB, W), lambda k, code, where, tiles, j=j: (tiles[j], 0)) for j in range(NB)] + [HELD] * 2,
        (block, other, near, swapped, far) + (top,) * NB + (high, low),
        f32(W, W), [pltpu.VMEM((W, W), F32), pltpu.VMEM((W, W), F32), pltpu.SemaphoreType.DMA((2,))],
    )
    near_s = after(near_s, far_s)
    swapped_s = lax.ppermute(near_s, "leaf", swap)
    other_s = lax.ppermute(sigma_a, "leaf", swap)
    slabs_b = call(
        lower_sum_kernel, "lower_sum", (code, where), [ANY] * 5 + [HELD] * 3,
        (sigma_a, other_s, near_s, swapped_s, far_s, p, high, low), [f32(W, TB)] * 4,
        [pltpu.VMEM((W, TB), F32), pltpu.VMEM((W, W), F32), pltpu.SemaphoreType.DMA],
    )
    own, next_one, opposite, last_one = to_owners(slabs_b, count)
    sigma_b = dinv_b + ((own + next_one) + (opposite + last_one))[None, None]
    return sigma_a[None], sigma_b


def solution(mesh):
    in_specs = (
        P(None, "tile"),
        P("leaf", None),
        P("leaf", None, None),
        P("leaf", None, "tile"),
        P("leaf"),
        P("leaf", None, None),
        P("leaf", None, None, None),
        P("leaf", None, None, None),
        P("leaf", None, None, "tile"),
    )
    out_specs = (P("leaf", None, "tile"), P("leaf", None, None, "tile"))
    return jax.shard_map(body, mesh=mesh, in_specs=in_specs, out_specs=out_specs, check_vma=False)
```

```python
import jax
import jax.numpy as jnp
from jax import lax
from jax.experimental import pallas as pl
from jax.experimental.pallas import tpu as pltpu
from jax.sharding import PartitionSpec as P

TB = 128
WT = 4
NA = 12
NB = 8
W = 512
SA = 1536
SB = 1536
OWN = 4
HALF = 256
SENT = HALF + 8
BLOCK = 2 * SENT
CHUNKS = 3
F32 = jnp.float32
BF16 = jnp.bfloat16
FIRST = ((0,), (0,))
PLAIN = ((1,), (0,))
ANY = pl.BlockSpec(memory_space=pl.ANY)


def split(x):
    high = x.astype(BF16)
    return high, (x - high.astype(F32)).astype(BF16)


def dot3(a, b, contract):
    left = jnp.concatenate([a[0], a[0], a[1]], axis=contract[0][0])
    right = jnp.concatenate([b[0], b[1], b[0]], axis=contract[1][0])
    return lax.dot_general(left, right, (contract, ((), ())), preferred_element_type=F32)


HELD = pl.BlockSpec(memory_space=pltpu.VMEM)


def whole(*shape):
    return pl.BlockSpec(shape, lambda *_: (0,) * len(shape))


def call(kernel, name, scalars, in_specs, operands, out_shapes, scratch=(), limit=24, out=HELD):
    many = isinstance(out_shapes, list)
    out_specs = [out] * len(out_shapes) if many else out
    return pl.pallas_call(
        kernel,
        grid_spec=pltpu.PrefetchScalarGridSpec(
            num_scalar_prefetch=len(scalars),
            grid=(1,),
            in_specs=in_specs,
            out_specs=out_specs,
            scratch_shapes=list(scratch),
        ),
        out_shape=out_shapes,
        compiler_params=pltpu.CompilerParams(vmem_limit_bytes=limit << 20),
        cost_estimate=pl.CostEstimate(flops=1 << 20, bytes_accessed=1 << 16, transcendentals=0),
        name=name,
    )(*scalars, *operands)


def f32(*shape):
    return jax.ShapeDtypeStruct(shape, F32)


def bf16(*shape):
    return jax.ShapeDtypeStruct(shape, BF16)


def place_among(tiles, count, tile):
    at, there = jnp.int32(0), jnp.int32(0)
    for j in range(count):
        same = (tiles(j) == tile).astype(jnp.int32)
        at, there = at + j * same, there + same
    return at, there


def store_slabs(full, place, slabs):
    for r in range(OWN):
        start = pl.multiple_of(lax.rem(place + r, OWN) * TB, TB)
        slabs[r][...] = full[:, pl.ds(start, TB)]


def halves(core):
    mine = pl.ds(pl.multiple_of(core * HALF, HALF), HALF)
    rest = pl.ds(pl.multiple_of((1 - core) * HALF, HALF), HALF)
    return mine, rest


def upper_rows_kernel(anc, parent, others_parent, where, top, u_ref, block, rows, factor, total, row_sems, u_sems):
    per = NA // CHUNKS
    size = per * TB

    def u_copy(c):
        part = pl.ds(c * size, size)
        return pltpu.make_async_copy(u_ref.at[0, part, :], factor.at[part, :], u_sems.at[c])

    def row_copy(j):
        start = pl.multiple_of(anc[0, j] * TB, TB)
        return pltpu.make_async_copy(top.at[pl.ds(start, TB), :], rows.at[pl.ds(j * TB, TB), :], row_sems.at[j])

    for c in range(CHUNKS):
        u_copy(c).start()
        for i in range(per):
            row_copy(c * per + i).start()
    for c in range(CHUNKS):
        u_copy(c).wait()
        for i in range(per):
            row_copy(c * per + i).wait()
        part = slice(c * size, (c + 1) * size)
        product = dot3(split(factor[part, :]), split(rows[part, :]), FIRST)
        if c == 0:
            total[...] = product
        else:
            total[...] += product
    for r in range(OWN):
        _, there = place_among(lambda j: anc[0, j], NA, where[0] * OWN + r)

        @pl.when(there == 0)
        def _():
            total[:, r * TB:(r + 1) * TB] = jnp.zeros((W, TB), F32)

    lane = lax.broadcasted_iota(jnp.int32, (SENT - HALF, W), 1)
    marks = jnp.where(lane == NA, parent[0], jnp.where(lane == NA + 1, others_parent[0], 0))
    for j in range(NA):
        marks = jnp.where(lane == j, anc[0, j], marks)
    for h in range(2):
        block[h * SENT:h * SENT + HALF, :] = total[h * HALF:(h + 1) * HALF, :]
        block[h * SENT + HALF:(h + 1) * SENT, :] = marks.astype(F32)


def upper_sum_kernel(anc, where, block, u_ref, s0, s1, s2, s3, tiles, full, sems):
    def copy(r, at):
        rows = pl.ds(pl.multiple_of(at * TB, TB), TB)
        return pltpu.make_async_copy(u_ref.at[0, rows, :], tiles.at[pl.ds(r * TB, TB), :], sems.at[r])

    found = [place_among(lambda j: anc[0, j], NA, where[0] * OWN + r) for r in range(OWN)]
    for r in range(OWN):
        copy(r, found[r][0]).start()
    for r in range(OWN):
        copy(r, found[r][0]).wait()
    own = split(
        jnp.concatenate(
            [jnp.where(found[r][1] > 0, tiles[r * TB:(r + 1) * TB, :], 0.0) for r in range(OWN)], axis=0
        )
    )
    for h in range(2):
        full[h * HALF:(h + 1) * HALF, :] = dot3(split(block[h * SENT:h * SENT + HALF, :]), own, PLAIN)
    store_slabs(full, where[0], (s0, s1, s2, s3))


def lower_prepare_kernel(pattern, u_ref, high, low):
    for i in range(WT + NB):
        for j in range(WT):
            rows, cols = slice(i * TB, (i + 1) * TB), slice(j * TB, (j + 1) * TB)
            masked = u_ref[0, 0, rows, cols] * pattern[i * WT + j].astype(F32)
            high[rows, cols], low[rows, cols] = split(masked)


def after_kernel(array, earlier, same):
    pass


def after(array, earlier):
    return pl.pallas_call(
        after_kernel,
        in_specs=[ANY, ANY],
        out_specs=ANY,
        out_shape=jax.ShapeDtypeStruct(array.shape, array.dtype),
        input_output_aliases={0: 0},
        compiler_params=pltpu.CompilerParams(vmem_limit_bytes=1 << 20),
        cost_estimate=pl.CostEstimate(flops=1, bytes_accessed=1, transcendentals=0),
        name="after",
    )(array, earlier)


def take_marks_kernel(array, same, marks, sem):
    copy = pltpu.make_async_copy(array.at[pl.ds(HALF, SENT - HALF), :], marks, sem)
    copy.start()
    copy.wait()


def take_marks(array):
    return pl.pallas_call(
        take_marks_kernel,
        in_specs=[ANY],
        out_specs=[ANY, HELD],
        out_shape=[jax.ShapeDtypeStruct(array.shape, F32), f32(SENT - HALF, W)],
        scratch_shapes=[pltpu.SemaphoreType.DMA],
        input_output_aliases={0: 0},
        compiler_params=pltpu.CompilerParams(vmem_limit_bytes=1 << 20),
        cost_estimate=pl.CostEstimate(flops=1, bytes_accessed=1, transcendentals=0),
        name="take_marks",
    )(array)


def fetch(choice, copies):
    for c, some in enumerate(copies):
        @pl.when(choice == c)
        def _():
            for copy in some:
                copy.start()
            for copy in some:
                copy.wait()


def lower_cross_kernel(code, where, far_tiles, own, other, near, swapped, far, *refs):
    high, low, p_ref, block, value, sems = refs[NB:]
    mine, rest = halves(where[1])
    part = pl.ds(0, HALF)
    second = pl.ds(SENT, HALF)

    def full(ref):
        return [
            pltpu.make_async_copy(ref.at[part, :], block.at[pl.ds(0, HALF), :], sems.at[0]),
            pltpu.make_async_copy(ref.at[second, :], block.at[pl.ds(HALF, HALF), :], sems.at[1]),
        ]

    fetch(
        code[0],
        [
            full(own),
            full(other),
            [
                pltpu.make_async_copy(near.at[part, :], block.at[mine, :], sems.at[0]),
                pltpu.make_async_copy(swapped.at[part, :], block.at[rest, :], sems.at[1]),
            ],
            full(far),
        ],
    )
    rows = split(jnp.concatenate([g[...] for g in refs[:NB]], axis=0) * 0.5)
    value[...] = dot3((high[W:, :], low[W:, :]), rows, FIRST) - dot3((high[:W, :], low[:W, :]), split(block[...]), FIRST)
    own_high, own_low = [], []
    for r in range(OWN):
        at, there = place_among(lambda j: far_tiles[j], NB, where[0] * OWN + r)

        @pl.when(there == 0)
        def _():
            value[:, r * TB:(r + 1) * TB] = jnp.zeros((W, TB), F32)

        rows = pl.ds(pl.multiple_of(W + at * TB, TB), TB)
        own_high.append(high[rows, :])
        own_low.append(low[rows, :])
    rows_of_own = jnp.concatenate(own_high, axis=0), jnp.concatenate(own_low, axis=0)
    product = dot3(split(value[...]), rows_of_own, PLAIN)
    p_ref[...] = product + product.T


def lower_sum_kernel(code, where, own, even, near, swapped, far, p_ref, high, low, s0, s1, s2, s3, block, full, sem):
    fetch(code[1], [[pltpu.make_async_copy(ref, block, sem)] for ref in (own, even, near, swapped, far)])
    inner = dot3(split(block[...]), (high[:W, :], low[:W, :]), FIRST)
    rows = pl.ds(pl.multiple_of(where[0] * TB, TB), TB)
    full[...] = p_ref[...] + dot3(split(inner), (high[rows, :], low[rows, :]), FIRST)
    store_slabs(full, where[0], (s0, s1, s2, s3))


def to_owners(slabs, count):
    ways = [[(i, (i + r) % count) for i in range(count)] for r in range(count)]
    arrived = [lax.ppermute(slabs[r], "tile", ways[r]) for r in (2, 1, 3)]
    return slabs[0], arrived[1], arrived[0], arrived[2]


def body(top, anc_a, u_a, dinv_a, parent, sel_b, pattern, u_b, dinv_b):
    leaves = lax.axis_size("leaf")
    count = lax.axis_size("tile")
    place = lax.axis_index("tile").astype(jnp.int32)
    leaf = lax.axis_index("leaf").astype(jnp.int32)
    core = leaf % 2
    even = core == 0
    where = jnp.stack([place, core, leaf])
    swap = [(i, i ^ 1) for i in range(leaves)]
    next_chip = [(i, i + 2) for i in range(leaves - 2)]
    crossing = [(i, (i + 2) ^ 1) for i in range(leaves - 2)]
    odd_on = [(i, i + 3) for i in range(1, leaves - 3, 2)]

    others_parent = lax.ppermute(parent, "leaf", swap)
    block = call(
        upper_rows_kernel, "upper_rows", (anc_a, parent, others_parent, where), [ANY, ANY], (top, u_a), f32(BLOCK, W),
        [pltpu.VMEM((SA, W), F32), pltpu.VMEM((SA, W), F32), pltpu.VMEM((W, W), F32),
         pltpu.SemaphoreType.DMA((NA,)), pltpu.SemaphoreType.DMA((CHUNKS,))], 48,
    )
    slabs_a = call(
        upper_sum_kernel, "upper_sum", (anc_a, where), [HELD, ANY], (block, u_a), [f32(W, TB)] * 4,
        [pltpu.VMEM((W, W), F32), pltpu.VMEM((W, W), F32), pltpu.SemaphoreType.DMA((OWN,))],
    )
    other = lax.ppermute(block, "leaf", swap)
    odd_heads = jnp.where(even, others_parent[0], parent[0]) == leaf - core + 1
    latest = jnp.where(
        jnp.logical_xor(even, odd_heads),
        lax.dynamic_slice_in_dim(block, core * SENT, SENT, 0),
        lax.dynamic_slice_in_dim(other, core * SENT, SENT, 0),
    )
    near = lax.ppermute(latest, "leaf", next_chip)
    far = lax.ppermute(block, "leaf", odd_on)

    high, low = call(
        lower_prepare_kernel, "lower_prepare", (pattern.reshape(-1),), [whole(1, 1, SB, W)], (u_b,), [bf16(SB, W)] * 2,
    )
    own, next_one, opposite, last_one = to_owners(slabs_a, count)
    sigma_a = dinv_a[0] + ((own + next_one) + (opposite + last_one))
    near_s = lax.ppermute(sigma_a, "leaf", crossing)
    far_s = lax.ppermute(sigma_a, "leaf", odd_on)

    head = parent[0]
    back = leaf - head
    from_far = jnp.logical_and(even, back == 3)
    from_even = jnp.logical_and(jnp.logical_not(even), back == 1)
    code_x = jnp.where(back == 0, 0, jnp.where(from_even, 1, jnp.where(from_far, 3, 2)))
    direct = jnp.where(head % 2 == 1 - core, 2, 3)
    code_s = jnp.where(back == 0, 0, jnp.where(from_even, 1, jnp.where(from_far, 4, direct)))
    code = jnp.stack([code_x, code_s]).astype(jnp.int32)

    near, near_marks = take_marks(after(near, sigma_a))
    swapped = lax.ppermute(near, "leaf", swap)
    own_marks = jnp.pad(anc_a.astype(F32), ((0, 0), (0, W - NA)))
    marked = jnp.where(
        code_x == 0, own_marks, jnp.where(code_x == 1, other[HALF:SENT], jnp.where(code_x == 3, far[HALF:SENT], near_marks))
    )[0, :NA].astype(jnp.int32)
    far_tiles = jnp.sum(
        jnp.where(sel_b[0, 0][:, None] == jnp.arange(NA, dtype=jnp.int32)[None], marked[None], 0), axis=1
    )
    p = call(
        lower_cross_kernel, "lower_cross", (code, where, far_tiles),
        [ANY] * 5 + [pl.BlockSpec((TB, W), lambda k, code, where, tiles, j=j: (tiles[j], 0)) for j in range(NB)] + [HELD] * 2,
        (block, other, near, swapped, far) + (top,) * NB + (high, low),
        f32(W, W), [pltpu.VMEM((W, W), F32), pltpu.VMEM((W, W), F32), pltpu.SemaphoreType.DMA((2,))],
    )
    near_s = after(near_s, far_s)
    swapped_s = lax.ppermute(near_s, "leaf", swap)
    other_s = lax.ppermute(sigma_a, "leaf", swap)
    slabs_b = call(
        lower_sum_kernel, "lower_sum", (code, where), [ANY] * 5 + [HELD] * 3,
        (sigma_a, other_s, near_s, swapped_s, far_s, p, high, low), [f32(W, TB)] * 4,
        [pltpu.VMEM((W, TB), F32), pltpu.VMEM((W, W), F32), pltpu.SemaphoreType.DMA],
    )
    own, next_one, opposite, last_one = to_owners(slabs_b, count)
    sigma_b = dinv_b + ((own + next_one) + (opposite + last_one))[None, None]
    return sigma_a[None], sigma_b


def solution(mesh):
    in_specs = (
        P(None, "tile"),
        P("leaf", None),
        P("leaf", None, None),
        P("leaf", None, "tile"),
        P("leaf"),
        P("leaf", None, None),
        P("leaf", None, None, None),
        P("leaf", None, None, None),
        P("leaf", None, None, "tile"),
    )
    out_specs = (P("leaf", None, "tile"), P("leaf", None, None, "tile"))
    return jax.shard_map(body, mesh=mesh, in_specs=in_specs, out_specs=out_specs, check_vma=False)
```

```python
import jax
import jax.numpy as jnp
from jax import lax
from jax.experimental import pallas as pl
from jax.experimental.pallas import tpu as pltpu
from jax.sharding import PartitionSpec as P

TB = 128
WT = 4
NA = 12
NB = 8
W = 512
SA = 1536
SB = 1536
OWN = 4
HALF = 256
SENT = HALF + 8
BLOCK = 2 * SENT
CHUNKS = 3
F32 = jnp.float32
BF16 = jnp.bfloat16
FIRST = ((0,), (0,))
PLAIN = ((1,), (0,))
ANY = pl.BlockSpec(memory_space=pl.ANY)


def split(x):
    high = x.astype(BF16)
    return high, (x - high.astype(F32)).astype(BF16)


def dot3(a, b, contract):
    left = jnp.concatenate([a[0], a[0], a[1]], axis=contract[0][0])
    right = jnp.concatenate([b[0], b[1], b[0]], axis=contract[1][0])
    return lax.dot_general(left, right, (contract, ((), ())), preferred_element_type=F32)


HELD = pl.BlockSpec(memory_space=pltpu.VMEM)


def whole(*shape):
    return pl.BlockSpec(shape, lambda *_: (0,) * len(shape))


def call(kernel, name, scalars, in_specs, operands, out_shapes, scratch=(), limit=24, out=HELD):
    many = isinstance(out_shapes, list)
    out_specs = [out] * len(out_shapes) if many else out
    return pl.pallas_call(
        kernel,
        grid_spec=pltpu.PrefetchScalarGridSpec(
            num_scalar_prefetch=len(scalars),
            grid=(1,),
            in_specs=in_specs,
            out_specs=out_specs,
            scratch_shapes=list(scratch),
        ),
        out_shape=out_shapes,
        compiler_params=pltpu.CompilerParams(vmem_limit_bytes=limit << 20),
        cost_estimate=pl.CostEstimate(flops=1 << 20, bytes_accessed=1 << 16, transcendentals=0),
        name=name,
    )(*scalars, *operands)


def f32(*shape):
    return jax.ShapeDtypeStruct(shape, F32)


def bf16(*shape):
    return jax.ShapeDtypeStruct(shape, BF16)


def place_among(tiles, count, tile):
    at, there = jnp.int32(0), jnp.int32(0)
    for j in range(count):
        same = (tiles(j) == tile).astype(jnp.int32)
        at, there = at + j * same, there + same
    return at, there


def store_slabs(full, place, slabs):
    for r in range(OWN):
        start = pl.multiple_of(lax.rem(place + r, OWN) * TB, TB)
        slabs[r][...] = full[:, pl.ds(start, TB)]


def halves(core):
    mine = pl.ds(pl.multiple_of(core * HALF, HALF), HALF)
    rest = pl.ds(pl.multiple_of((1 - core) * HALF, HALF), HALF)
    return mine, rest


def upper_rows_kernel(anc, parent, others_parent, where, top, u_ref, block, rows, factor, total, row_sems, u_sems):
    per = NA // CHUNKS
    size = per * TB

    def u_copy(c):
        part = pl.ds(c * size, size)
        return pltpu.make_async_copy(u_ref.at[0, part, :], factor.at[part, :], u_sems.at[c])

    def row_copy(j):
        start = pl.multiple_of(anc[0, j] * TB, TB)
        return pltpu.make_async_copy(top.at[pl.ds(start, TB), :], rows.at[pl.ds(j * TB, TB), :], row_sems.at[j])

    for c in range(CHUNKS):
        u_copy(c).start()
        for i in range(per):
            row_copy(c * per + i).start()
    for c in range(CHUNKS):
        u_copy(c).wait()
        for i in range(per):
            row_copy(c * per + i).wait()
        part = slice(c * size, (c + 1) * size)
        product = dot3(split(factor[part, :]), split(rows[part, :]), FIRST)
        if c == 0:
            total[...] = product
        else:
            total[...] += product
    for r in range(OWN):
        _, there = place_among(lambda j: anc[0, j], NA, where[0] * OWN + r)

        @pl.when(there == 0)
        def _():
            total[:, r * TB:(r + 1) * TB] = jnp.zeros((W, TB), F32)

    lane = lax.broadcasted_iota(jnp.int32, (SENT - HALF, W), 1)
    marks = jnp.where(lane == NA, parent[0], jnp.where(lane == NA + 1, others_parent[0], 0))
    for j in range(NA):
        marks = jnp.where(lane == j, anc[0, j], marks)
    for h in range(2):
        block[h * SENT:h * SENT + HALF, :] = total[h * HALF:(h + 1) * HALF, :]
        block[h * SENT + HALF:(h + 1) * SENT, :] = marks.astype(F32)


def upper_sum_kernel(anc, where, block, u_ref, s0, s1, s2, s3, tiles, full, sems):
    def copy(r, at):
        rows = pl.ds(pl.multiple_of(at * TB, TB), TB)
        return pltpu.make_async_copy(u_ref.at[0, rows, :], tiles.at[pl.ds(r * TB, TB), :], sems.at[r])

    found = [place_among(lambda j: anc[0, j], NA, where[0] * OWN + r) for r in range(OWN)]
    for r in range(OWN):
        copy(r, found[r][0]).start()
    for r in range(OWN):
        copy(r, found[r][0]).wait()
    own = split(
        jnp.concatenate(
            [jnp.where(found[r][1] > 0, tiles[r * TB:(r + 1) * TB, :], 0.0) for r in range(OWN)], axis=0
        )
    )
    for h in range(2):
        full[h * HALF:(h + 1) * HALF, :] = dot3(split(block[h * SENT:h * SENT + HALF, :]), own, PLAIN)
    store_slabs(full, where[0], (s0, s1, s2, s3))


def lower_prepare_kernel(pattern, u_ref, high, low):
    for i in range(WT + NB):
        for j in range(WT):
            rows, cols = slice(i * TB, (i + 1) * TB), slice(j * TB, (j + 1) * TB)
            masked = u_ref[0, 0, rows, cols] * pattern[i * WT + j].astype(F32)
            high[rows, cols], low[rows, cols] = split(masked)


def after_kernel(array, earlier, same):
    pass


def after(array, earlier):
    return pl.pallas_call(
        after_kernel,
        in_specs=[ANY, ANY],
        out_specs=ANY,
        out_shape=jax.ShapeDtypeStruct(array.shape, array.dtype),
        input_output_aliases={0: 0},
        compiler_params=pltpu.CompilerParams(vmem_limit_bytes=1 << 20),
        cost_estimate=pl.CostEstimate(flops=1, bytes_accessed=1, transcendentals=0),
        name="after",
    )(array, earlier)


def take_marks_kernel(array, same, marks, sem):
    copy = pltpu.make_async_copy(array.at[pl.ds(HALF, SENT - HALF), :], marks, sem)
    copy.start()
    copy.wait()


def take_marks(array):
    return pl.pallas_call(
        take_marks_kernel,
        in_specs=[ANY],
        out_specs=[ANY, HELD],
        out_shape=[jax.ShapeDtypeStruct(array.shape, F32), f32(SENT - HALF, W)],
        scratch_shapes=[pltpu.SemaphoreType.DMA],
        input_output_aliases={0: 0},
        compiler_params=pltpu.CompilerParams(vmem_limit_bytes=1 << 20),
        cost_estimate=pl.CostEstimate(flops=1, bytes_accessed=1, transcendentals=0),
        name="take_marks",
    )(array)


def fetch(choice, copies):
    for c, some in enumerate(copies):
        @pl.when(choice == c)
        def _():
            for copy in some:
                copy.start()
            for copy in some:
                copy.wait()


def lower_cross_kernel(code, where, far_tiles, own, other, near, swapped, far, *refs):
    high, low, p_ref, block, value, sems = refs[NB:]
    mine, rest = halves(where[1])
    part = pl.ds(0, HALF)
    second = pl.ds(SENT, HALF)

    def full(ref):
        return [
            pltpu.make_async_copy(ref.at[part, :], block.at[pl.ds(0, HALF), :], sems.at[0]),
            pltpu.make_async_copy(ref.at[second, :], block.at[pl.ds(HALF, HALF), :], sems.at[1]),
        ]

    fetch(
        code[0],
        [
            full(own),
            full(other),
            [
                pltpu.make_async_copy(near.at[part, :], block.at[mine, :], sems.at[0]),
                pltpu.make_async_copy(swapped.at[part, :], block.at[rest, :], sems.at[1]),
            ],
            full(far),
        ],
    )
    rows = split(jnp.concatenate([g[...] for g in refs[:NB]], axis=0) * 0.5)
    value[...] = dot3((high[W:, :], low[W:, :]), rows, FIRST) - dot3((high[:W, :], low[:W, :]), split(block[...]), FIRST)
    own_high, own_low = [], []
    for r in range(OWN):
        at, there = place_among(lambda j: far_tiles[j], NB, where[0] * OWN + r)

        @pl.when(there == 0)
        def _():
            value[:, r * TB:(r + 1) * TB] = jnp.zeros((W, TB), F32)

        rows = pl.ds(pl.multiple_of(W + at * TB, TB), TB)
        own_high.append(high[rows, :])
        own_low.append(low[rows, :])
    rows_of_own = jnp.concatenate(own_high, axis=0), jnp.concatenate(own_low, axis=0)
    product = dot3(split(value[...]), rows_of_own, PLAIN)
    p_ref[...] = product + product.T


def lower_sum_kernel(code, where, own, even, near, swapped, far, p_ref, high, low, s0, s1, s2, s3, block, full, sem):
    fetch(code[1], [[pltpu.make_async_copy(ref, block, sem)] for ref in (own, even, near, swapped, far)])
    inner = dot3(split(block[...]), (high[:W, :], low[:W, :]), FIRST)
    rows = pl.ds(pl.multiple_of(where[0] * TB, TB), TB)
    full[...] = p_ref[...] + dot3(split(inner), (high[rows, :], low[rows, :]), FIRST)
    store_slabs(full, where[0], (s0, s1, s2, s3))


def to_owners(slabs, count):
    ways = [[(i, (i + r) % count) for i in range(count)] for r in range(count)]
    arrived = [lax.ppermute(slabs[r], "tile", ways[r]) for r in (2, 1, 3)]
    return slabs[0], arrived[0], arrived[1], arrived[2]


def body(top, anc_a, u_a, dinv_a, parent, sel_b, pattern, u_b, dinv_b):
    leaves = lax.axis_size("leaf")
    count = lax.axis_size("tile")
    place = lax.axis_index("tile").astype(jnp.int32)
    leaf = lax.axis_index("leaf").astype(jnp.int32)
    core = leaf % 2
    even = core == 0
    where = jnp.stack([place, core, leaf])
    swap = [(i, i ^ 1) for i in range(leaves)]
    next_chip = [(i, i + 2) for i in range(leaves - 2)]
    crossing = [(i, (i + 2) ^ 1) for i in range(leaves - 2)]
    odd_on = [(i, i + 3) for i in range(1, leaves - 3, 2)]

    others_parent = lax.ppermute(parent, "leaf", swap)
    block = call(
        upper_rows_kernel, "upper_rows", (anc_a, parent, others_parent, where), [ANY, ANY], (top, u_a), f32(BLOCK, W),
        [pltpu.VMEM((SA, W), F32), pltpu.VMEM((SA, W), F32), pltpu.VMEM((W, W), F32),
         pltpu.SemaphoreType.DMA((NA,)), pltpu.SemaphoreType.DMA((CHUNKS,))], 48,
    )
    slabs_a = call(
        upper_sum_kernel, "upper_sum", (anc_a, where), [HELD, ANY], (block, u_a), [f32(W, TB)] * 4,
        [pltpu.VMEM((W, W), F32), pltpu.VMEM((W, W), F32), pltpu.SemaphoreType.DMA((OWN,))],
    )
    other = lax.ppermute(block, "leaf", swap)
    odd_heads = jnp.where(even, others_parent[0], parent[0]) == leaf - core + 1
    latest = jnp.where(
        jnp.logical_xor(even, odd_heads),
        lax.dynamic_slice_in_dim(block, core * SENT, SENT, 0),
        lax.dynamic_slice_in_dim(other, core * SENT, SENT, 0),
    )
    near = lax.ppermute(latest, "leaf", next_chip)
    far = lax.ppermute(block, "leaf", odd_on)

    high, low = call(
        lower_prepare_kernel, "lower_prepare", (pattern.reshape(-1),), [whole(1, 1, SB, W)], (u_b,), [bf16(SB, W)] * 2,
    )
    own, next_one, opposite, last_one = to_owners(slabs_a, count)
    sigma_a = dinv_a[0] + ((own + next_one) + (opposite + last_one))
    near_s = lax.ppermute(sigma_a, "leaf", crossing)
    far_s = lax.ppermute(sigma_a, "leaf", odd_on)

    head = parent[0]
    back = leaf - head
    from_far = jnp.logical_and(even, back == 3)
    from_even = jnp.logical_and(jnp.logical_not(even), back == 1)
    code_x = jnp.where(back == 0, 0, jnp.where(from_even, 1, jnp.where(from_far, 3, 2)))
    direct = jnp.where(head % 2 == 1 - core, 2, 3)
    code_s = jnp.where(back == 0, 0, jnp.where(from_even, 1, jnp.where(from_far, 4, direct)))
    code = jnp.stack([code_x, code_s]).astype(jnp.int32)

    near, near_marks = take_marks(after(near, sigma_a))
    swapped = lax.ppermute(near, "leaf", swap)
    own_marks = jnp.pad(anc_a.astype(F32), ((0, 0), (0, W - NA)))
    marked = jnp.where(
        code_x == 0, own_marks, jnp.where(code_x == 1, other[HALF:SENT], jnp.where(code_x == 3, far[HALF:SENT], near_marks))
    )[0, :NA].astype(jnp.int32)
    far_tiles = jnp.sum(
        jnp.where(sel_b[0, 0][:, None] == jnp.arange(NA, dtype=jnp.int32)[None], marked[None], 0), axis=1
    )
    p = call(
        lower_cross_kernel, "lower_cross", (code, where, far_tiles),
        [ANY] * 5 + [pl.BlockSpec((TB, W), lambda k, code, where, tiles, j=j: (tiles[j], 0)) for j in range(NB)] + [HELD] * 2,
        (block, other, near, swapped, far) + (top,) * NB + (high, low),
        f32(W, W), [pltpu.VMEM((W, W), F32), pltpu.VMEM((W, W), F32), pltpu.SemaphoreType.DMA((2,))],
    )
    near_s = after(near_s, far_s)
    swapped_s = lax.ppermute(near_s, "leaf", swap)
    other_s = lax.ppermute(sigma_a, "leaf", swap)
    slabs_b = call(
        lower_sum_kernel, "lower_sum", (code, where), [ANY] * 5 + [HELD] * 3,
        (sigma_a, other_s, near_s, swapped_s, far_s, p, high, low), [f32(W, TB)] * 4,
        [pltpu.VMEM((W, TB), F32), pltpu.VMEM((W, W), F32), pltpu.SemaphoreType.DMA],
    )
    own, next_one, opposite, last_one = to_owners(slabs_b, count)
    sigma_b = dinv_b + ((own + next_one) + (opposite + last_one))[None, None]
    return sigma_a[None], sigma_b


def solution(mesh):
    in_specs = (
        P(None, "tile"),
        P("leaf", None),
        P("leaf", None, None),
        P("leaf", None, "tile"),
        P("leaf"),
        P("leaf", None, None),
        P("leaf", None, None, None),
        P("leaf", None, None, None),
        P("leaf", None, None, "tile"),
    )
    out_specs = (P("leaf", None, "tile"), P("leaf", None, None, "tile"))
    return jax.shard_map(body, mesh=mesh, in_specs=in_specs, out_specs=out_specs, check_vma=False)
```
